256 devices in a mesh: replica: 8 (over z_lo, x), fsdp: 32 (over y, z_hi, core).
Axes of the slice: x: 4, y: 4, z: 8 (z_hi: 4, z_lo: 2; z = z_hi * 2 + z_lo), core: 2. Of those that a mesh axis runs over, the one named last changes fastest.
Arguments:
- hidden_in: bfloat16 [8, 12288, 8192], P('replica', 'fsdp'), may hold values from -6 to 6
- value_weight: bfloat16 [8, 8192, 512], P('replica', 'fsdp'), may hold values from -0.0625 to 0.0625
- grad_out: bfloat16 [8, 12288, 512], P('replica', 'fsdp'), may hold values from -0.0546875 to 0.0546875
- local_fragment: float32 [8, 8388608], P('replica', 'fsdp'), may hold values from -6 to 6
- global_fragment: float32 [8388608], P('fsdp'), may hold values from -6 to 6
- momentum: float32 [8388608], P('fsdp'), may hold values from -3 to 3
- residual: float32 [8, 8388608], P('replica', 'fsdp'), may hold values from -3 to 3
Outputs:
- values: bfloat16 [8, 12288, 512], P('replica', 'fsdp')
- weight_grad: float32 [8, 8192, 512], P('replica', 'fsdp')
- mixed_fragment: float32 [8, 8388608], P('replica', 'fsdp')
- new_momentum: float32 [8388608], P('fsdp')
The draws below stay inside these ranges and needn't reach their ends.
All inputs are finite; a program needn't handle non-finite values.
Results may differ from the reference program's by a relative error of at most 0.015.
Values may be sent and summed in bfloat16 or wider, within the bound.
No kernel may reach another device: no remote copies, remote signals or barrier semaphores. Data moves between devices by JAX's collectives and lax.ppermute only.
A program may use at most 128 MiB of HBM per device.

```python
import jax
import jax.numpy as jnp
from jax import lax

D = 8192
BLOCK = 128
KVW = 512
REPLICAS = 8
GROUP_TOK = 12288
FRAG = 8388608


def spiked(entries, key, source, target, blocks, factor):
    def block_of(dim):
        return (jnp.arange(entries.shape[dim]) // (entries.shape[dim] // blocks)).reshape((-1,) + (1,) * (entries.ndim - 1 - dim))

    one_side = jax.random.permutation(key, blocks)[block_of(target)]
    far = (block_of(target) + blocks // 2) % blocks
    return jnp.where((block_of(source) == one_side) | (block_of(source) == far), factor * entries, entries)


def level_of(stream_key, dims, cuts, least, largest):
    gain, own = 1.0, jax.random.fold_in(stream_key, 6)
    for dim, blocks in cuts:
        draws = jnp.exp(jax.random.uniform(jax.random.fold_in(own, dim), (blocks,), jnp.float32, least / len(cuts), largest / len(cuts)))
        gain = gain * jnp.repeat(draws, dims[dim] // blocks).reshape([-1 if axis == dim else 1 for axis in range(len(dims))])
    return gain


def scatter_about(key, extent, width, reach, cuts=(), kind=jnp.bfloat16):
    entries = width * jax.random.normal(key, extent, jnp.float32)
    if cuts:
        entries = entries * level_of(key, extent, cuts, -0.22, 0.18)
    return jnp.clip(entries, -reach, reach).astype(kind)


def noise_with(own_key, dims, deviation, most, pieces, heavy, kind=jnp.bfloat16):
    result = deviation * jax.random.normal(own_key, dims, jnp.float32)
    if pieces:
        result = result * level_of(own_key, dims, pieces, -0.22, 0.18)
    return jnp.clip(spiked(result, jax.random.fold_in(own_key, 3), *heavy), -most, most).astype(kind)


def setup_inputs(seed: int = 0) -> dict:
    key_list = jax.random.split(jax.random.key(seed), 8)
    hidden_in = noise_with(key_list[0], (REPLICAS, GROUP_TOK, D), 1.0, 6.0, ((0, 8), (1, 32)), (1, 2, 32, 2.75))
    value_weight = scatter_about(key_list[1], (REPLICAS, D, KVW), D ** -0.5, 0.0625, ((0, 8), (1, 32)))
    grad_out = scatter_about(key_list[2], (REPLICAS, GROUP_TOK, KVW), GROUP_TOK ** -0.5, 0.0546875, ((0, 8), (1, 32)))
    local_fragment = scatter_about(key_list[3], (REPLICAS, FRAG), 1.0, 6.0, ((0, 8), (1, 32)), jnp.float32)
    global_fragment = scatter_about(key_list[4], (FRAG,), 1.0, 6.0, ((0, 32),), jnp.float32)
    momentum = scatter_about(key_list[5], (FRAG,), 0.5, 3.0, ((0, 32),), jnp.float32)
    residual = scatter_about(key_list[6], (REPLICAS, FRAG), 0.5, 3.0, ((0, 8), (1, 32)), jnp.float32)
    return {"hidden_in": hidden_in, "value_weight": value_weight, "grad_out": grad_out, "local_fragment": local_fragment, "global_fragment": global_fragment, "momentum": momentum, "residual": residual}


outer_rate = 0.7
outer_momentum = 0.9
mix_weight = 0.5


def replica_step(triple):
    tokens, weight, cotangent = triple
    projected = jnp.dot(tokens, weight, preferred_element_type=jnp.float32).astype(jnp.bfloat16)
    gradient = lax.dot_general(tokens, cotangent, (((0,), (0,)), ((), ())), preferred_element_type=jnp.float32)
    return projected, gradient


def reference(hidden_in, value_weight, grad_out, local_fragment, global_fragment, momentum, residual):
    values, weight_grad = lax.map(replica_step, (hidden_in, value_weight, grad_out))
    nudged = (global_fragment[None, :] - local_fragment) + residual
    blocks = nudged.reshape(REPLICAS, FRAG // BLOCK, BLOCK)
    block_scale = lax.optimization_barrier((jnp.max(jnp.abs(blocks), axis=2) + 1e-6).astype(jnp.bfloat16))
    scale_wide = block_scale.astype(jnp.float32)[:, :, None]
    block_codes = lax.optimization_barrier((blocks / scale_wide).astype(jnp.bfloat16))
    decoded = block_codes.astype(jnp.float32) * scale_wide
    average = (jnp.sum(decoded, axis=0) / REPLICAS).reshape(FRAG)
    new_momentum = outer_momentum * momentum + average
    new_global = global_fragment - outer_rate * (average + outer_momentum * new_momentum)
    mixed_fragment = mix_weight * local_fragment + (1.0 - mix_weight) * new_global[None, :]
    return values, weight_grad, mixed_fragment, new_momentum
```

```python
import functools

import jax
import jax.numpy as jnp
from jax import lax
from jax.experimental import pallas as pl
from jax.experimental.pallas import tpu as pltpu
from jax.sharding import Mesh, PartitionSpec as P

BLOCK = 128


outer_rate = 0.7
outer_momentum = 0.9
mix_weight = 0.5

RING = 4
ROWS = 256


def shift(v, axis, k):
    n = lax.axis_size(axis)
    return lax.ppermute(v, axis, [(i, (i + k) % n) for i in range(n)])


def params(mib=32):
    return pltpu.CompilerParams(vmem_limit_bytes=mib << 20)


def pick_kernel(_, h_ref, o_ref):
    o_ref[...] = h_ref[...]


def other_columns(tokens, core):
    t, d = tokens.shape
    n = d // (2 * ROWS)
    return pl.pallas_call(
        pick_kernel,
        grid_spec=pltpu.PrefetchScalarGridSpec(
            num_scalar_prefetch=1,
            grid=(n,),
            in_specs=[pl.BlockSpec((t, ROWS), lambda i, s: (0, 2 * i + 1 - s[0]))],
            out_specs=pl.BlockSpec((t, ROWS), lambda i, s: (0, i)),
        ),
        out_shape=jax.ShapeDtypeStruct((t, d // 2), tokens.dtype),
        compiler_params=params(),
        cost_estimate=pl.CostEstimate(flops=0, bytes_accessed=2 * t * d, transcendentals=0),
    )(core[None], tokens)


TN = (((0,), (0,)), ((), ()))


def grad_kernel(n, naccs, _, h_ref, hr_ref, g_ref, gp_ref, *refs):
    accs, outs = refs[: 2 * naccs], refs[2 * naccs :]
    i = pl.program_id(0)
    total = lax.dot_general(h_ref[...], g_ref[...], TN, preferred_element_type=jnp.float32)
    total += lax.dot_general(hr_ref[...], gp_ref[...], TN, preferred_element_type=jnp.float32)
    for half in range(2):

        @pl.when((i < n // 2) if half == 0 else (i >= n // 2))
        def _():
            s = total
            for a in range(naccs):
                s = s + accs[2 * a + half][0].astype(jnp.float32)
            outs[half][0] = s.astype(outs[half].dtype)


def grad_blocks(core, blocks, tokens, theirs, cot, cot_theirs, accs, dtype):
    t = tokens.shape[0]
    k = cot.shape[1]
    n = blocks.shape[0]
    h = n // 2
    first = lambda i, s: (jnp.minimum(i, h - 1), 0, 0)
    second = lambda i, s: (jnp.maximum(i - h, 0), 0, 0)
    unit = (1, ROWS, k)
    return pl.pallas_call(
        functools.partial(grad_kernel, n, len(accs)),
        grid_spec=pltpu.PrefetchScalarGridSpec(
            num_scalar_prefetch=1,
            grid=(n,),
            in_specs=[
                pl.BlockSpec((t, ROWS), lambda i, s: (0, 2 * s[i + 1] + s[0])),
                pl.BlockSpec((t, ROWS), lambda i, s: (0, s[i + 1])),
                pl.BlockSpec((t, k), lambda i, s: (0, 0)),
                pl.BlockSpec((t, k), lambda i, s: (0, 0)),
            ]
            + [pl.BlockSpec(unit, first), pl.BlockSpec(unit, second)] * len(accs),
            out_specs=[pl.BlockSpec(unit, first), pl.BlockSpec(unit, second)],
        ),
        out_shape=[jax.ShapeDtypeStruct((h, ROWS, k), dtype)] * 2,
        compiler_params=params(),
        cost_estimate=pl.CostEstimate(
            flops=4 * n * ROWS * t * k, bytes_accessed=n * ROWS * (4 * t + 4 * k), transcendentals=0
        ),
    )(
        jnp.concatenate([core[None], blocks]),
        tokens,
        theirs,
        cot,
        cot_theirs,
        *[a for pair in accs for a in pair],
    )


def values_kernel(n, has_acc, _, *refs):
    pieces, h, hr = refs[:n], refs[n : 2 * n], refs[2 * n : 3 * n]
    outs = refs[-2:]
    for j, blocks in enumerate((h, hr)):
        total = refs[3 * n + j][...] if has_acc else None
        for piece, block in zip(pieces, blocks):
            part = jnp.dot(block[...], piece[...], preferred_element_type=jnp.float32)
            total = part if total is None else total + part
        outs[j][...] = total


def values_part(core, pieces, tokens, theirs, acc):
    t = tokens.shape[0]
    k = pieces[0][0].shape[1]
    n = len(pieces)
    specs, ours, other = [], [], []
    for j, (w, _, half) in enumerate(pieces):
        r = w.shape[0]
        f = ROWS // r
        half = half or 0
        specs.append(pl.BlockSpec((r, k), lambda i, s: (0, 0)))
        ours.append(
            pl.BlockSpec((t, r), lambda i, s, j=j, f=f, half=half: (0, (2 * s[j + 1] + s[0]) * f + half))
        )
        other.append(pl.BlockSpec((t, r), lambda i, s, j=j, f=f, half=half: (0, s[j + 1] * f + half)))
    whole = pl.BlockSpec((t, k), lambda i, s: (0, 0))
    rows = sum(w.shape[0] for w, _, _ in pieces)
    acc = list(acc or ())
    return pl.pallas_call(
        functools.partial(values_kernel, n, bool(acc)),
        grid_spec=pltpu.PrefetchScalarGridSpec(
            num_scalar_prefetch=1,
            grid=(1,),
            in_specs=specs + ours + other + [whole] * len(acc),
            out_specs=[whole, whole],
        ),
        out_shape=[jax.ShapeDtypeStruct((t, k), jnp.float32)] * 2,
        compiler_params=params(48),
        cost_estimate=pl.CostEstimate(
            flops=4 * t * rows * k, bytes_accessed=4 * t * rows + 2 * rows * k, transcendentals=0
        ),
    )(
        jnp.stack([core] + [b for _, b, _ in pieces]),
        *[w for w, _, _ in pieces],
        *[tokens] * n,
        *[theirs] * n,
        *acc,
    )


def per_device(
    hidden_in, value_weight, grad_out, local_fragment, global_fragment, momentum, residual
):
    tokens = hidden_in[0]
    weight = value_weight[0]
    cot = grad_out[0]
    x, y, zh, core = (lax.axis_index(a) for a in ("x", "y", "zh", "core"))

    def block(dy, dz):
        return lax.rem(y + dy, RING) * RING + lax.rem(zh + dz, RING)

    cot_theirs = shift(cot, "core", 1)
    theirs = shift(other_columns(tokens, core), "core", 1)

    hw = ROWS // 2

    def spread(v, axis):
        h = v.shape[0] // 2
        prev, nxt = shift(v, axis, 1), shift(v, axis, -1)
        return prev, nxt, shift(prev[:h], axis, 1), shift(nxt[h:], axis, -1)

    z3, z1, z2a, z2b = spread(weight, "zh")
    groups = [
        (weight, [0]),
        (jnp.concatenate([z1, z3]), [1, 3]),
        (jnp.concatenate([z2a, z2b]), [2]),
    ]
    near, mid, far = [], [], []
    for v, zs in groups:
        prev, nxt, fa, fb = spread(v, "y")
        for j, dz in enumerate(zs):
            cut = slice(j * ROWS, (j + 1) * ROWS)
            near.append((v[cut], block(0, dz), None))
            mid.append((prev[cut], block(3, dz), None))
            mid.append((nxt[cut], block(1, dz), None))
        if len(zs) == 1:
            far += [(fa, block(2, zs[0]), 0), (fb, block(2, zs[0]), 1)]
        else:
            far += [(fa, block(2, zs[0]), None), (fb, block(2, zs[1]), None)]

    local_row = local_fragment[0]
    nudged = global_fragment - local_row + residual[0]
    blocks = nudged.reshape(-1, BLOCK)
    block_scale = lax.optimization_barrier(
        (jnp.max(jnp.abs(blocks), axis=1) + 1e-06).astype(jnp.bfloat16)
    )
    block_codes = lax.optimization_barrier(
        (blocks / block_scale.astype(jnp.float32)[:, None]).astype(jnp.bfloat16)
    )
    decoded = block_codes.astype(jnp.float32) * block_scale.astype(jnp.float32)[:, None]
    decoded = decoded.astype(jnp.bfloat16)
    part = decoded.shape[0] // RING

    def chunk(k):
        return lax.dynamic_slice_in_dim(decoded, lax.rem(x + k, RING) * part, part)

    parts = [chunk(0)] + [shift(chunk(k), "x", k) for k in (1, 2, 3)]
    over_x = sum(v.astype(jnp.float32) for v in parts).astype(jnp.bfloat16)
    both = over_x.astype(jnp.float32) + shift(over_x, "zl", 1).astype(jnp.float32)
    mine = both.astype(jnp.bfloat16)
    ordered = jnp.concatenate([mine] + [shift(mine, "x", -k) for k in (1, 2, 3)])
    ordered = jnp.concatenate([ordered, ordered])
    summed_all = lax.dynamic_slice_in_dim(
        ordered, lax.rem(RING - x, RING) * part, RING * part
    ).astype(jnp.float32)
    replicas = lax.axis_size("x") * lax.axis_size("zl")
    average = (summed_all / replicas).reshape(-1)
    new_momentum = outer_momentum * momentum + average
    new_global = global_fragment - outer_rate * (average + outer_momentum * new_momentum)
    mixed_fragment = mix_weight * local_row + (1.0 - mix_weight) * new_global

    def grads(where, accs, dtype):
        return grad_blocks(
            core, jnp.stack([block(*w) for w in where]), tokens, theirs, cot, cot_theirs, accs, dtype
        )

    bf = jnp.bfloat16
    far_a, far_b = grads([(2, 0), (2, 1), (2, 2), (2, 3)], [], bf)
    in_a, in_b = shift(far_a, "y", 1), shift(far_b, "y", -1)
    dir_b, dir_a = grads([(1, 2), (1, 3), (3, 0), (3, 1)], [], bf)
    got_b, got_a = shift(dir_b, "y", 1), shift(dir_a, "y", -1)
    mer_a, mer_b = grads([(1, 0), (1, 1), (3, 2), (3, 3)], [(in_a, in_b)], bf)
    sum_a, sum_b = shift(mer_a, "y", 1), shift(mer_b, "y", -1)
    s01, s23 = grads(
        [(0, 0), (0, 1), (0, 2), (0, 3)], [(got_a, got_b), (sum_a, sum_b)], jnp.float32
    )
    s0, s1, s2, s3 = s01[0], s01[1], s23[0], s23[1]
    in_a, in_b = shift(s2[:hw].astype(bf), "zh", 1), shift(s2[hw:].astype(bf), "zh", -1)
    got_b, got_a = shift(s1[hw:].astype(bf), "zh", 1), shift(s3[:hw].astype(bf), "zh", -1)
    f32 = jnp.float32
    sum_a = shift((s1[:hw] + in_a.astype(f32)).astype(bf), "zh", 1)
    sum_b = shift((s3[hw:] + in_b.astype(f32)).astype(bf), "zh", -1)
    top = s0[:hw] + got_a.astype(f32) + sum_a.astype(f32)
    bottom = s0[hw:] + got_b.astype(f32) + sum_b.astype(f32)
    grad_rows = jnp.concatenate([top, bottom])

    acc = values_part(core, near, tokens, theirs, None)
    acc = values_part(core, mid, tokens, theirs, acc)
    ours, other = values_part(core, far, tokens, theirs, acc)
    values = (ours + shift(other, "core", 1)).astype(bf)

    return (values[None], grad_rows[None], mixed_fragment[None], new_momentum)


def solution(mesh):
    whole = Mesh(mesh.devices.reshape(2, 4, 4, 4, 2), ("zl", "x", "y", "zh", "core"))
    replica, fsdp = ("zl", "x"), ("y", "zh", "core")
    return jax.shard_map(
        per_device,
        mesh=whole,
        in_specs=(
            P(replica, fsdp, None),
            P(replica, fsdp, None),
            P(replica, fsdp, None),
            P(replica, fsdp),
            P(fsdp),
            P(fsdp),
            P(replica, fsdp),
        ),
        out_specs=(
            P(replica, fsdp, None),
            P(replica, fsdp, None),
            P(replica, fsdp),
            P(fsdp),
        ),
        check_vma=False,
    )
```

```python
import functools

import jax
import jax.numpy as jnp
from jax import lax
from jax.experimental import pallas as pl
from jax.experimental.pallas import tpu as pltpu
from jax.sharding import Mesh, PartitionSpec as P

BLOCK = 128


outer_rate = 0.7
outer_momentum = 0.9
mix_weight = 0.5

RING = 4
ROWS = 256


def shift(v, axis, k):
    n = lax.axis_size(axis)
    return lax.ppermute(v, axis, [(i, (i + k) % n) for i in range(n)])


def params(mib=24):
    return pltpu.CompilerParams(vmem_limit_bytes=mib << 20)


FREE = pl.CostEstimate(flops=1, bytes_accessed=1, transcendentals=0)
TN = (((0,), (0,)), ((), ()))
PAIR = 2 * ROWS

FAR = [(2, 0), (2, 1), (2, 2), (2, 3)]
NEXT = [(1, 2), (1, 3), (3, 0), (3, 1)]
LAST = [(1, 0), (1, 1), (3, 2), (3, 3), (0, 0), (0, 1), (0, 2), (0, 3)]


def after(v, *others):
    return lax.optimization_barrier((v, *others))[0]


def pick_kernel(n, s_ref, a_ref, b_ref, *refs):
    (*cots, mine, send), core = refs, s_ref[0]
    i = pl.program_id(0)

    def pair():
        for j, v in enumerate((a_ref, b_ref)):
            cut = slice(j * ROWS, (j + 1) * ROWS)
            left, right = v[:, :ROWS], v[:, ROWS:]
            mine[:, cut] = jnp.where(core == 0, left, right)
            send[:, cut] = jnp.where(core == 0, right, left)

    if not cots:
        pair()
        return
    pl.when(i < n)(pair)

    @pl.when(i == n)
    def _():
        send[...] = cots[0][...]


def pick(tokens, core, blocks, cot=None):
    t = tokens.shape[0]
    n = len(blocks) // 2
    cots = [] if cot is None else [cot]
    steps = n + len(cots)
    return pl.pallas_call(
        functools.partial(pick_kernel, n),
        grid_spec=pltpu.PrefetchScalarGridSpec(
            num_scalar_prefetch=1,
            grid=(steps,),
            in_specs=[
                pl.BlockSpec((t, PAIR), lambda i, s, j=j: (0, s[2 * jnp.minimum(i, n - 1) + j + 1]))
                for j in range(2)
            ]
            + [pl.BlockSpec((t, PAIR), lambda i, s: (0, 0))] * len(cots),
            out_specs=[
                pl.BlockSpec((t, PAIR), lambda i, s: (0, jnp.minimum(i, n - 1))),
                pl.BlockSpec((t, PAIR), lambda i, s: (0, i)),
            ],
        ),
        out_shape=[
            jax.ShapeDtypeStruct((t, n * PAIR), tokens.dtype),
            jax.ShapeDtypeStruct((t, steps * PAIR), tokens.dtype),
        ],
        compiler_params=params(),
        cost_estimate=FREE,
    )(jnp.stack([core] + blocks), tokens, tokens, *cots)


def stack_kernel(*refs):
    out = refs[-1]
    r = refs[0].shape[0]
    for i, v in enumerate(refs[:-1]):
        out[i * r : (i + 1) * r] = v[...]


def stack_rows(*arrays):
    r, k = arrays[0].shape
    n = len(arrays)
    return pl.pallas_call(
        stack_kernel,
        out_shape=jax.ShapeDtypeStruct((n * r, k), arrays[0].dtype),
        compiler_params=params(),
        cost_estimate=FREE,
    )(*arrays)


def grad_kernel(h_ref, hr_ref, g_ref, gp_ref, *outs):
    total = lax.dot_general(h_ref[...], g_ref[...], TN, preferred_element_type=jnp.float32)
    total += lax.dot_general(hr_ref[...], gp_ref[...], TN, preferred_element_type=jnp.float32)
    for step, out in enumerate(outs):

        @pl.when(pl.program_id(0) == step)
        def _():
            out[...] = total.astype(out.dtype)


def grad_rows_of(mine, theirs, first, cot, with_cot, dtypes):
    t, k = cot.shape
    column = pl.BlockSpec((t, PAIR), lambda i: (0, i + first))
    last = with_cot.shape[1] // k - 1
    return pl.pallas_call(
        grad_kernel,
        grid=(len(dtypes),),
        in_specs=[
            column,
            column,
            pl.BlockSpec((t, k), lambda i: (0, 0)),
            pl.BlockSpec((t, k), lambda i: (0, last)),
        ],
        out_specs=[pl.BlockSpec((PAIR, k), lambda i: (0, 0))] * len(dtypes),
        out_shape=[jax.ShapeDtypeStruct((PAIR, k), d) for d in dtypes],
        compiler_params=params(),
        cost_estimate=FREE,
    )(mine, theirs, cot, with_cot)


def sums_kernel(own_01, own_23, a, b, c, d, s0, s1, s2, s3):
    f32 = jnp.float32
    for j, out in enumerate((s0, s1, s2, s3)):
        own, more = ((own_01, (a, b)), (own_23, (c, d)))[j // 2]
        cut = slice((j % 2) * ROWS, (j % 2 + 1) * ROWS)
        out[...] = (own[cut] + more[0][cut].astype(f32) + more[1][cut].astype(f32)).astype(out.dtype)


def sums_along_y(own_01, own_23, *received):
    k = own_01.shape[1]
    dtypes = [jnp.float32] + [jnp.bfloat16] * 3
    return pl.pallas_call(
        sums_kernel,
        out_shape=[jax.ShapeDtypeStruct((ROWS, k), d) for d in dtypes],
        compiler_params=params(),
        cost_estimate=FREE,
    )(own_01, own_23, *received)


def values_kernel(cuts, has_acc, *refs):
    m, n = len(cuts), sum(len(c) for c in cuts)
    pieces, h, hr = refs[:m], refs[m : m + n], refs[m + n : m + 2 * n]
    outs = refs[-2:]
    for j, blocks in enumerate((h, hr)):
        total = refs[m + 2 * n + j][...] if has_acc else None
        b = 0
        for piece, cut in zip(pieces, cuts):
            for start in cut:
                part = jnp.dot(
                    blocks[b][...],
                    piece[start : start + PAIR],
                    preferred_element_type=jnp.float32,
                )
                total = part if total is None else total + part
                b += 1
        outs[j][...] = total


def values_part(pieces, acc):
    cuts = [[start for start, _, _ in parts] for _, parts in pieces]
    use = [(source, pair) for _, parts in pieces for _, source, pair in parts]
    t = use[0][0][0].shape[0]
    k = pieces[0][0].shape[1]
    acc = list(acc or ())
    whole = pl.BlockSpec((t, k), lambda i: (0, 0))
    columns = [pl.BlockSpec((t, PAIR), lambda i, p=p: (0, p)) for _, p in use]
    return pl.pallas_call(
        functools.partial(values_kernel, cuts, bool(acc)),
        grid=(1,),
        in_specs=[pl.BlockSpec(w.shape, lambda i: (0, 0)) for w, _ in pieces]
        + columns
        + columns
        + [whole] * len(acc),
        out_specs=[whole, whole],
        out_shape=[jax.ShapeDtypeStruct((t, k), jnp.float32)] * 2,
        compiler_params=params(),
        cost_estimate=FREE,
    )(
        *[w for w, _ in pieces],
        *[source[0] for source, _ in use],
        *[source[1] for source, _ in use],
        *acc,
    )


def encode_kernel(_, l_ref, g_ref, r_ref, *outs):
    nudged = (g_ref[...] - l_ref[...]) + r_ref[...]
    top = jnp.max(jnp.abs(nudged), axis=1, keepdims=True) + 1e-06
    scale = top.astype(jnp.bfloat16).astype(jnp.float32)
    codes = (nudged / scale).astype(jnp.bfloat16).astype(jnp.float32)
    decoded = (codes * scale).astype(jnp.bfloat16)
    for k, out in enumerate(outs):

        @pl.when(pl.program_id(0) == k)
        def _():
            out[...] = decoded


def encode(x, local_row, global_row, residual_row):
    n = local_row.shape[0] // RING
    part = pl.BlockSpec((n, BLOCK), lambda i, s: (lax.rem(s[0] + i, RING), 0))
    return pl.pallas_call(
        encode_kernel,
        grid_spec=pltpu.PrefetchScalarGridSpec(
            num_scalar_prefetch=1,
            grid=(RING,),
            in_specs=[part] * 3,
            out_specs=[pl.BlockSpec((n, BLOCK), lambda i, s: (0, 0))] * RING,
        ),
        out_shape=[jax.ShapeDtypeStruct((n, BLOCK), jnp.bfloat16)] * RING,
        compiler_params=params(),
        cost_estimate=FREE,
    )(x[None], local_row, global_row, residual_row)


def outer_kernel(replicas, _, l_ref, g_ref, m_ref, *refs):
    sums, (mixed_ref, momentum_ref) = refs[:-2], refs[-2:]
    for k, chunk in enumerate(sums):

        @pl.when(pl.program_id(0) == k)
        def _():
            average = chunk[...].astype(jnp.float32) / replicas
            new_momentum = outer_momentum * m_ref[...] + average
            new_global = g_ref[...] - outer_rate * (average + outer_momentum * new_momentum)
            mixed_ref[...] = mix_weight * l_ref[...] + (1.0 - mix_weight) * new_global
            momentum_ref[...] = new_momentum


def outer_step(x, replicas, local_row, global_row, momentum_row, sums):
    n = local_row.shape[0] // RING
    part = pl.BlockSpec((n, BLOCK), lambda i, s: (lax.rem(s[0] + i, RING), 0))
    return pl.pallas_call(
        functools.partial(outer_kernel, replicas),
        grid_spec=pltpu.PrefetchScalarGridSpec(
            num_scalar_prefetch=1,
            grid=(RING,),
            in_specs=[part] * 3 + [pl.BlockSpec((n, BLOCK), lambda i, s: (0, 0))] * RING,
            out_specs=[part, part],
        ),
        out_shape=[jax.ShapeDtypeStruct(local_row.shape, jnp.float32)] * 2,
        compiler_params=params(),
        cost_estimate=FREE,
    )(x[None], local_row, global_row, momentum_row, *sums)


def per_device(
    hidden_in, value_weight, grad_out, local_fragment, global_fragment, momentum, residual
):
    tokens = hidden_in[0]
    weight = value_weight[0]
    cot = grad_out[0]
    bf, f32 = jnp.bfloat16, jnp.float32
    x, y, zh, core = (lax.axis_index(a) for a in ("x", "y", "zh", "core"))

    def blocks(where):
        return [lax.rem(y + dy, RING) * RING + lax.rem(zh + dz, RING) for dy, dz in where]

    w_1, w_3 = shift(weight, "zh", -1), shift(weight, "zh", -3)

    mine, send = pick(tokens, core, blocks(FAR + NEXT + LAST), cot)
    local_row, global_row, momentum_row, residual_row = (
        v.reshape(-1, BLOCK) for v in (local_fragment, global_fragment, momentum, residual)
    )
    chunks = encode(x, local_row, global_row, residual_row)
    mine, send, w_1, w_3, *chunks = lax.optimization_barrier((mine, send, w_1, w_3, *chunks))
    theirs = shift(send, "core", 1)
    parts = [chunks[0]] + [shift(chunks[k], "x", k) for k in (1, 2, 3)]

    w_2 = shift(after(weight, w_1), "zh", 2)
    w_01 = stack_rows(weight, w_1)
    prev_01, next_01 = shift(w_01, "y", 1), shift(w_01, "y", -1)

    def grads(first, dtypes, *others):
        return grad_rows_of(mine, after(theirs, *others), first, cot, theirs, dtypes)

    far_a, far_b = grads(0, [bf, bf], w_01)
    in_a, in_b = shift(far_a, "y", 1), shift(far_b, "y", -1)
    parts = after(tuple(parts), far_a)
    dir_b, dir_a = grads(2, [bf, bf], *parts)
    over_x = sum(v.astype(f32) for v in after(parts, dir_b)).astype(bf)
    from_zl = shift(over_x, "zl", 1)
    got_b, got_a = shift(dir_b, "y", 1), shift(dir_a, "y", -1)

    in_a, in_b, from_zl = lax.optimization_barrier((in_a, in_b, from_zl, dir_b))[:3]
    own_a, own_b, own_01, own_23 = grads(4, [f32] * 4, in_a, in_b, from_zl)
    prev_01, next_01 = after((prev_01, next_01), own_a)
    far_01 = shift(prev_01, "y", 1)
    in_a, in_b, next_01 = lax.optimization_barrier((in_a, in_b, next_01))
    mer_a = (own_a + in_a.astype(f32)).astype(bf)
    mer_b = (own_b + in_b.astype(f32)).astype(bf)
    sum_a, sum_b = shift(mer_a, "y", 1), shift(mer_b, "y", -1)

    from_zl, over_x = after((from_zl, over_x), mer_a, mer_b)
    total = (over_x.astype(f32) + from_zl.astype(f32)).astype(bf)
    totals = [total] + [shift(total, "x", -k) for k in (1, 2, 3)]
    replicas = lax.axis_size("x") * lax.axis_size("zl")
    mixed, new_momentum = outer_step(x, replicas, local_row, global_row, momentum_row, totals)

    w_23 = stack_rows(*after((w_2, w_3), mixed))
    received = after((got_a, sum_a, got_b, sum_b), w_23, mixed)
    s0, s1, s2, s3 = sums_along_y(own_01, own_23, *received)
    g1, g2, g3 = (shift(v, "zh", k) for v, k in ((s1, 1), (s2, 2), (s3, 3)))
    w_23 = after(w_23, s1)
    prev_23, next_23 = shift(w_23, "y", 1), shift(w_23, "y", -1)

    cols = (mine, theirs)
    acc = values_part(
        [
            (after(w_01, s1), [(0, cols, 6)]),
            (w_23, [(0, cols, 7)]),
            (prev_01, [(0, cols, 3)]),
            (next_01, [(0, cols, 4)]),
            (far_01, [(0, cols, 0)]),
        ],
        None,
    )
    prev_23, next_23 = after((prev_23, next_23), acc[0], g1, g3)
    far_23 = shift(next_23, "y", -1)
    acc = values_part([(prev_23, [(0, cols, 5)]), (next_23, [(0, cols, 2)])], acc)
    far_23, g1, g2, g3 = lax.optimization_barrier((far_23, g1, g2, g3))
    ours, other = values_part([(far_23, [(0, cols, 1)])], acc)
    back = shift(other, "core", 1)
    grad_rows = s0 + g1.astype(f32) + g2.astype(f32) + g3.astype(f32)
    values = (ours + back).astype(bf)

    return (values[None], grad_rows[None], mixed.reshape(1, -1), new_momentum.reshape(-1))


def solution(mesh):
    whole = Mesh(mesh.devices.reshape(2, 4, 4, 4, 2), ("zl", "x", "y", "zh", "core"))
    replica, fsdp = ("zl", "x"), ("y", "zh", "core")
    return jax.shard_map(
        per_device,
        mesh=whole,
        in_specs=(
            P(replica, fsdp, None),
            P(replica, fsdp, None),
            P(replica, fsdp, None),
            P(replica, fsdp),
            P(fsdp),
            P(fsdp),
            P(replica, fsdp),
        ),
        out_specs=(
            P(replica, fsdp, None),
            P(replica, fsdp, None),
            P(replica, fsdp),
            P(fsdp),
        ),
        check_vma=False,
    )
```

```python
import functools

import jax
import jax.numpy as jnp
from jax import lax
from jax.experimental import pallas as pl
from jax.experimental.pallas import tpu as pltpu
from jax.sharding import Mesh, PartitionSpec as P

BLOCK = 128


outer_rate = 0.7
outer_momentum = 0.9
mix_weight = 0.5

RING = 4
ROWS = 256


def shift(v, axis, k):
    n = lax.axis_size(axis)
    return lax.ppermute(v, axis, [(i, (i + k) % n) for i in range(n)])


def params(mib=24):
    return pltpu.CompilerParams(vmem_limit_bytes=mib << 20)


FREE = pl.CostEstimate(flops=1, bytes_accessed=1, transcendentals=0)
TN = (((0,), (0,)), ((), ()))
PAIR = 2 * ROWS

FAR = [(2, 0), (2, 1), (2, 2), (2, 3)]
NEXT = [(1, 2), (1, 3), (3, 0), (3, 1)]
LAST = [(1, 0), (1, 1), (3, 2), (3, 3), (0, 0), (0, 1), (0, 2), (0, 3)]


def after(v, *others):
    return lax.optimization_barrier((v, *others))[0]


def pick_kernel(n, s_ref, a_ref, b_ref, *refs):
    (*cots, mine, send), core = refs, s_ref[0]
    i = pl.program_id(0)

    def pair():
        for j, v in enumerate((a_ref, b_ref)):
            cut = slice(j * ROWS, (j + 1) * ROWS)
            left, right = v[:, :ROWS], v[:, ROWS:]
            mine[:, cut] = jnp.where(core == 0, left, right)
            send[:, cut] = jnp.where(core == 0, right, left)

    if not cots:
        pair()
        return
    pl.when(i < n)(pair)

    @pl.when(i == n)
    def _():
        send[...] = cots[0][...]


def pick(tokens, core, blocks, cot=None):
    t = tokens.shape[0]
    n = len(blocks) // 2
    cots = [] if cot is None else [cot]
    steps = n + len(cots)
    return pl.pallas_call(
        functools.partial(pick_kernel, n),
        grid_spec=pltpu.PrefetchScalarGridSpec(
            num_scalar_prefetch=1,
            grid=(steps,),
            in_specs=[
                pl.BlockSpec((t, PAIR), lambda i, s, j=j: (0, s[2 * jnp.minimum(i, n - 1) + j + 1]))
                for j in range(2)
            ]
            + [pl.BlockSpec((t, PAIR), lambda i, s: (0, 0))] * len(cots),
            out_specs=[
                pl.BlockSpec((t, PAIR), lambda i, s: (0, jnp.minimum(i, n - 1))),
                pl.BlockSpec((t, PAIR), lambda i, s: (0, i)),
            ],
        ),
        out_shape=[
            jax.ShapeDtypeStruct((t, n * PAIR), tokens.dtype),
            jax.ShapeDtypeStruct((t, steps * PAIR), tokens.dtype),
        ],
        compiler_params=params(),
        cost_estimate=FREE,
    )(jnp.stack([core] + blocks), tokens, tokens, *cots)


def stack_kernel(*refs):
    out = refs[-1]
    r = refs[0].shape[0]
    for i, v in enumerate(refs[:-1]):
        out[i * r : (i + 1) * r] = v[...]


def stack_rows(*arrays):
    r, k = arrays[0].shape
    n = len(arrays)
    return pl.pallas_call(
        stack_kernel,
        out_shape=jax.ShapeDtypeStruct((n * r, k), arrays[0].dtype),
        compiler_params=params(),
        cost_estimate=FREE,
    )(*arrays)


def grad_kernel(h_ref, hr_ref, g_ref, gp_ref, *outs):
    total = lax.dot_general(h_ref[...], g_ref[...], TN, preferred_element_type=jnp.float32)
    total += lax.dot_general(hr_ref[...], gp_ref[...], TN, preferred_element_type=jnp.float32)
    for step, out in enumerate(outs):

        @pl.when(pl.program_id(0) == step)
        def _():
            out[...] = total.astype(out.dtype)


def grad_rows_of(mine, theirs, first, cot, with_cot, dtypes):
    t, k = cot.shape
    column = pl.BlockSpec((t, PAIR), lambda i: (0, i + first))
    last = with_cot.shape[1] // k - 1
    return pl.pallas_call(
        grad_kernel,
        grid=(len(dtypes),),
        in_specs=[
            column,
            column,
            pl.BlockSpec((t, k), lambda i: (0, 0)),
            pl.BlockSpec((t, k), lambda i: (0, last)),
        ],
        out_specs=[pl.BlockSpec((PAIR, k), lambda i: (0, 0))] * len(dtypes),
        out_shape=[jax.ShapeDtypeStruct((PAIR, k), d) for d in dtypes],
        compiler_params=params(),
        cost_estimate=FREE,
    )(mine, theirs, cot, with_cot)


def sums_kernel(own_01, own_23, a, b, c, d, up, down, own_up, own_down, own):
    f32 = jnp.float32
    h = ROWS // 2

    def half(j):
        mine, more = ((own_01, (a, b)), (own_23, (c, d)))[j // 4]
        cut = slice((j % 4) * h, (j % 4 + 1) * h)
        return mine[cut] + more[0][cut].astype(f32) + more[1][cut].astype(f32)

    own[:h], own[h:] = half(0), half(1)
    own_up[...], own_down[...] = half(2), half(7)
    up[:h], up[h:] = half(4).astype(up.dtype), half(3).astype(up.dtype)
    down[:h], down[h:] = half(5).astype(down.dtype), half(6).astype(down.dtype)


def sums_along_y(own_01, own_23, *received):
    k = own_01.shape[1]
    shapes = [(ROWS, jnp.bfloat16)] * 2 + [(ROWS // 2, jnp.float32)] * 2 + [(ROWS, jnp.float32)]
    return pl.pallas_call(
        sums_kernel,
        out_shape=[jax.ShapeDtypeStruct((r, k), d) for r, d in shapes],
        compiler_params=params(),
        cost_estimate=FREE,
    )(own_01, own_23, *received)


def values_kernel(cuts, has_acc, *refs):
    m, n = len(cuts), sum(len(c) for c in cuts)
    pieces, h, hr = refs[:m], refs[m : m + n], refs[m + n : m + 2 * n]
    outs = refs[-2:]
    for j, blocks in enumerate((h, hr)):
        total = refs[m + 2 * n + j][...] if has_acc else None
        b = 0
        for piece, cut in zip(pieces, cuts):
            for start in cut:
                part = jnp.dot(
                    blocks[b][...],
                    piece[start : start + PAIR],
                    preferred_element_type=jnp.float32,
                )
                total = part if total is None else total + part
                b += 1
        outs[j][...] = total


def values_part(pieces, acc):
    cuts = [[start for start, _, _ in parts] for _, parts in pieces]
    use = [(source, pair) for _, parts in pieces for _, source, pair in parts]
    t = use[0][0][0].shape[0]
    k = pieces[0][0].shape[1]
    acc = list(acc or ())
    whole = pl.BlockSpec((t, k), lambda i: (0, 0))
    columns = [pl.BlockSpec((t, PAIR), lambda i, p=p: (0, p)) for _, p in use]
    return pl.pallas_call(
        functools.partial(values_kernel, cuts, bool(acc)),
        grid=(1,),
        in_specs=[pl.BlockSpec(w.shape, lambda i: (0, 0)) for w, _ in pieces]
        + columns
        + columns
        + [whole] * len(acc),
        out_specs=[whole, whole],
        out_shape=[jax.ShapeDtypeStruct((t, k), jnp.float32)] * 2,
        compiler_params=params(),
        cost_estimate=FREE,
    )(
        *[w for w, _ in pieces],
        *[source[0] for source, _ in use],
        *[source[1] for source, _ in use],
        *acc,
    )


def encode_kernel(_, l_ref, g_ref, r_ref, *outs):
    nudged = (g_ref[...] - l_ref[...]) + r_ref[...]
    top = jnp.max(jnp.abs(nudged), axis=1, keepdims=True) + 1e-06
    scale = top.astype(jnp.bfloat16).astype(jnp.float32)
    codes = (nudged / scale).astype(jnp.bfloat16).astype(jnp.float32)
    decoded = (codes * scale).astype(jnp.bfloat16)
    for k, out in enumerate(outs):

        @pl.when(pl.program_id(0) == k)
        def _():
            out[...] = decoded


def encode(x, local_row, global_row, residual_row):
    n = local_row.shape[0] // RING
    part = pl.BlockSpec((n, BLOCK), lambda i, s: (lax.rem(s[0] + i, RING), 0))
    return pl.pallas_call(
        encode_kernel,
        grid_spec=pltpu.PrefetchScalarGridSpec(
            num_scalar_prefetch=1,
            grid=(RING,),
            in_specs=[part] * 3,
            out_specs=[pl.BlockSpec((n, BLOCK), lambda i, s: (0, 0))] * RING,
        ),
        out_shape=[jax.ShapeDtypeStruct((n, BLOCK), jnp.bfloat16)] * RING,
        compiler_params=params(),
        cost_estimate=FREE,
    )(x[None], local_row, global_row, residual_row)


def outer_kernel(replicas, _, l_ref, g_ref, m_ref, *refs):
    sums, (mixed_ref, momentum_ref) = refs[:-2], refs[-2:]
    for k, chunk in enumerate(sums):

        @pl.when(pl.program_id(0) == k)
        def _():
            average = chunk[...].astype(jnp.float32) / replicas
            new_momentum = outer_momentum * m_ref[...] + average
            new_global = g_ref[...] - outer_rate * (average + outer_momentum * new_momentum)
            mixed_ref[...] = mix_weight * l_ref[...] + (1.0 - mix_weight) * new_global
            momentum_ref[...] = new_momentum


def outer_step(x, replicas, local_row, global_row, momentum_row, sums):
    n = local_row.shape[0] // RING
    part = pl.BlockSpec((n, BLOCK), lambda i, s: (lax.rem(s[0] + i, RING), 0))
    return pl.pallas_call(
        functools.partial(outer_kernel, replicas),
        grid_spec=pltpu.PrefetchScalarGridSpec(
            num_scalar_prefetch=1,
            grid=(RING,),
            in_specs=[part] * 3 + [pl.BlockSpec((n, BLOCK), lambda i, s: (0, 0))] * RING,
            out_specs=[part, part],
        ),
        out_shape=[jax.ShapeDtypeStruct(local_row.shape, jnp.float32)] * 2,
        compiler_params=params(),
        cost_estimate=FREE,
    )(x[None], local_row, global_row, momentum_row, *sums)


def per_device(
    hidden_in, value_weight, grad_out, local_fragment, global_fragment, momentum, residual
):
    tokens = hidden_in[0]
    weight = value_weight[0]
    cot = grad_out[0]
    bf, f32 = jnp.bfloat16, jnp.float32
    x, y, zh, core = (lax.axis_index(a) for a in ("x", "y", "zh", "core"))

    def blocks(where):
        return [lax.rem(y + dy, RING) * RING + lax.rem(zh + dz, RING) for dy, dz in where]

    w_1, w_3 = shift(weight, "zh", -1), shift(weight, "zh", -3)

    mine, send = pick(tokens, core, blocks(FAR + NEXT + LAST), cot)
    local_row, global_row, momentum_row, residual_row = (
        v.reshape(-1, BLOCK) for v in (local_fragment, global_fragment, momentum, residual)
    )
    chunks = encode(x, local_row, global_row, residual_row)
    mine, send, w_1, w_3, *chunks = lax.optimization_barrier((mine, send, w_1, w_3, *chunks))
    theirs = shift(send, "core", 1)
    parts = [chunks[0]] + [shift(chunks[k], "x", k) for k in (1, 2, 3)]

    w_2 = shift(after(weight, w_1), "zh", 2)
    w_01 = stack_rows(weight, w_1)
    prev_01, next_01 = shift(w_01, "y", 1), shift(w_01, "y", -1)

    def grads(first, dtypes, *others):
        return grad_rows_of(mine, after(theirs, *others), first, cot, theirs, dtypes)

    far_a, far_b = grads(0, [bf, bf], w_01)
    in_a, in_b = shift(far_a, "y", 1), shift(far_b, "y", -1)
    parts = after(tuple(parts), far_a)
    dir_b, dir_a = grads(2, [bf, bf], *parts)
    over_x = sum(v.astype(f32) for v in after(parts, dir_b)).astype(bf)
    from_zl = shift(over_x, "zl", 1)
    got_b, got_a = shift(dir_b, "y", 1), shift(dir_a, "y", -1)

    in_a, in_b, from_zl = lax.optimization_barrier((in_a, in_b, from_zl, dir_b))[:3]
    own_a, own_b, own_01, own_23 = grads(4, [f32] * 4, in_a, in_b, from_zl)
    prev_01, next_01 = after((prev_01, next_01), own_a)
    far_01 = shift(prev_01, "y", 1)
    in_a, in_b, got_a, got_b, w_2 = lax.optimization_barrier((in_a, in_b, got_a, got_b, w_2))
    mer_a = (own_a + in_a.astype(f32)).astype(bf)
    mer_b = (own_b + in_b.astype(f32)).astype(bf)
    sum_a, sum_b = shift(mer_a, "y", 1), shift(mer_b, "y", -1)

    from_zl, over_x = after((from_zl, over_x), mer_a, mer_b)
    total = (over_x.astype(f32) + from_zl.astype(f32)).astype(bf)
    totals = [total] + [shift(total, "x", -k) for k in (1, 2, 3)]
    replicas = lax.axis_size("x") * lax.axis_size("zl")
    mixed, new_momentum = outer_step(x, replicas, local_row, global_row, momentum_row, totals)

    w_23 = stack_rows(*after((w_2, w_3), mixed))
    far_01, *received = lax.optimization_barrier((far_01, got_a, sum_a, got_b, sum_b, w_23, mixed))[:5]
    up, down, own_up, own_down, own = sums_along_y(own_01, own_23, *received)
    from_below, from_above = shift(up, "zh", 1), shift(down, "zh", -1)
    w_23 = after(w_23, up)
    prev_23, next_23 = shift(w_23, "y", 1), shift(w_23, "y", -1)

    cols = (mine, theirs)
    acc = values_part(
        [
            (after(w_01, up), [(0, cols, 6)]),
            (w_23, [(0, cols, 7)]),
            (prev_01, [(0, cols, 3)]),
            (next_01, [(0, cols, 4)]),
            (far_01, [(0, cols, 0)]),
        ],
        None,
    )
    h = ROWS // 2
    mer_up = (own_up + from_below[:h].astype(f32)).astype(bf)
    mer_down = (own_down + from_above[:h].astype(f32)).astype(bf)
    top, bottom = shift(mer_up, "zh", 1), shift(mer_down, "zh", -1)
    prev_23, next_23 = after((prev_23, next_23), acc[0], mer_up, mer_down)
    far_23 = shift(next_23, "y", -1)
    acc = values_part([(prev_23, [(0, cols, 5)]), (next_23, [(0, cols, 2)])], acc)
    far_23, top, bottom = lax.optimization_barrier((far_23, top, bottom))
    ours, other = values_part([(far_23, [(0, cols, 1)])], acc)
    back = shift(other, "core", 1)
    direct = jnp.concatenate([from_above[h:], from_below[h:]]).astype(f32)
    grad_rows = own + direct + jnp.concatenate([top, bottom]).astype(f32)
    values = (ours + back).astype(bf)

    return (values[None], grad_rows[None], mixed.reshape(1, -1), new_momentum.reshape(-1))


def solution(mesh):
    whole = Mesh(mesh.devices.reshape(2, 4, 4, 4, 2), ("zl", "x", "y", "zh", "core"))
    replica, fsdp = ("zl", "x"), ("y", "zh", "core")
    return jax.shard_map(
        per_device,
        mesh=whole,
        in_specs=(
            P(replica, fsdp, None),
            P(replica, fsdp, None),
            P(replica, fsdp, None),
            P(replica, fsdp),
            P(fsdp),
            P(fsdp),
            P(replica, fsdp),
        ),
        out_specs=(
            P(replica, fsdp, None),
            P(replica, fsdp, None),
            P(replica, fsdp),
            P(fsdp),
        ),
        check_vma=False,
    )
```

```python
import functools

import jax
import jax.numpy as jnp
from jax import lax
from jax.experimental import pallas as pl
from jax.experimental.pallas import tpu as pltpu
from jax.sharding import Mesh, PartitionSpec as P

BLOCK = 128


outer_rate = 0.7
outer_momentum = 0.9
mix_weight = 0.5

RING = 4
ROWS = 256


def shift(v, axis, k):
    n = lax.axis_size(axis)
    return lax.ppermute(v, axis, [(i, (i + k) % n) for i in range(n)])


def swap_x(v, bits):
    return lax.ppermute(v, "x", [(i, i ^ bits) for i in range(RING)])


def params(mib=24):
    return pltpu.CompilerParams(vmem_limit_bytes=mib << 20)


FREE = pl.CostEstimate(flops=1, bytes_accessed=1, transcendentals=0)
TN = (((0,), (0,)), ((), ()))
PAIR = 2 * ROWS

FAR = [(2, 0), (2, 1), (2, 2), (2, 3)]
NEXT = [(1, 2), (1, 3), (3, 0), (3, 1)]
LAST = [(1, 0), (1, 1), (3, 2), (3, 3), (0, 0), (0, 1), (0, 2), (0, 3)]


def after(v, *others):
    return lax.optimization_barrier((v, *others))[0]


def pick_kernel(n, s_ref, a_ref, b_ref, *refs):
    (*cots, mine, send), core = refs, s_ref[0]
    i = pl.program_id(0)

    def pair():
        for j, v in enumerate((a_ref, b_ref)):
            cut = slice(j * ROWS, (j + 1) * ROWS)
            left, right = v[:, :ROWS], v[:, ROWS:]
            mine[:, cut] = jnp.where(core == 0, left, right)
            send[:, cut] = jnp.where(core == 0, right, left)

    if not cots:
        pair()
        return
    pl.when(i < n)(pair)

    @pl.when(i == n)
    def _():
        send[...] = cots[0][...]


def pick(tokens, core, blocks, cot=None):
    t = tokens.shape[0]
    n = len(blocks) // 2
    cots = [] if cot is None else [cot]
    steps = n + len(cots)
    return pl.pallas_call(
        functools.partial(pick_kernel, n),
        grid_spec=pltpu.PrefetchScalarGridSpec(
            num_scalar_prefetch=1,
            grid=(steps,),
            in_specs=[
                pl.BlockSpec((t, PAIR), lambda i, s, j=j: (0, s[2 * jnp.minimum(i, n - 1) + j + 1]))
                for j in range(2)
            ]
            + [pl.BlockSpec((t, PAIR), lambda i, s: (0, 0))] * len(cots),
            out_specs=[
                pl.BlockSpec((t, PAIR), lambda i, s: (0, jnp.minimum(i, n - 1))),
                pl.BlockSpec((t, PAIR), lambda i, s: (0, i)),
            ],
        ),
        out_shape=[
            jax.ShapeDtypeStruct((t, n * PAIR), tokens.dtype),
            jax.ShapeDtypeStruct((t, steps * PAIR), tokens.dtype),
        ],
        compiler_params=params(),
        cost_estimate=FREE,
    )(jnp.stack([core] + blocks), tokens, tokens, *cots)


def stack_kernel(*refs):
    out = refs[-1]
    r = refs[0].shape[0]
    for i, v in enumerate(refs[:-1]):
        out[i * r : (i + 1) * r] = v[...]


def stack_rows(*arrays):
    r, k = arrays[0].shape
    n = len(arrays)
    return pl.pallas_call(
        stack_kernel,
        out_shape=jax.ShapeDtypeStruct((n * r, k), arrays[0].dtype),
        compiler_params=params(),
        cost_estimate=FREE,
    )(*arrays)


def grad_kernel(h_ref, hr_ref, g_ref, gp_ref, *outs):
    total = lax.dot_general(h_ref[...], g_ref[...], TN, preferred_element_type=jnp.float32)
    total += lax.dot_general(hr_ref[...], gp_ref[...], TN, preferred_element_type=jnp.float32)
    for step, out in enumerate(outs):

        @pl.when(pl.program_id(0) == step)
        def _():
            out[...] = total.astype(out.dtype)


def grad_rows_of(mine, theirs, first, cot, with_cot, dtypes):
    t, k = cot.shape
    column = pl.BlockSpec((t, PAIR), lambda i: (0, i + first))
    last = with_cot.shape[1] // k - 1
    return pl.pallas_call(
        grad_kernel,
        grid=(len(dtypes),),
        in_specs=[
            column,
            column,
            pl.BlockSpec((t, k), lambda i: (0, 0)),
            pl.BlockSpec((t, k), lambda i: (0, last)),
        ],
        out_specs=[pl.BlockSpec((PAIR, k), lambda i: (0, 0))] * len(dtypes),
        out_shape=[jax.ShapeDtypeStruct((PAIR, k), d) for d in dtypes],
        compiler_params=params(),
        cost_estimate=FREE,
    )(mine, theirs, cot, with_cot)


def sums_kernel(own_01, own_23, a, b, c, d, up, down, own_up, own_down, own):
    f32 = jnp.float32
    h = ROWS // 2

    def half(j):
        mine, more = ((own_01, (a, b)), (own_23, (c, d)))[j // 4]
        cut = slice((j % 4) * h, (j % 4 + 1) * h)
        return mine[cut] + more[0][cut].astype(f32) + more[1][cut].astype(f32)

    own[:h], own[h:] = half(0), half(1)
    own_up[...], own_down[...] = half(2), half(7)
    up[:h], up[h:] = half(4).astype(up.dtype), half(3).astype(up.dtype)
    down[:h], down[h:] = half(5).astype(down.dtype), half(6).astype(down.dtype)


def sums_along_y(own_01, own_23, *received):
    k = own_01.shape[1]
    shapes = [(ROWS, jnp.bfloat16)] * 2 + [(ROWS // 2, jnp.float32)] * 2 + [(ROWS, jnp.float32)]
    return pl.pallas_call(
        sums_kernel,
        out_shape=[jax.ShapeDtypeStruct((r, k), d) for r, d in shapes],
        compiler_params=params(),
        cost_estimate=FREE,
    )(own_01, own_23, *received)


def values_kernel(cuts, has_acc, *refs):
    m, n = len(cuts), sum(len(c) for c in cuts)
    pieces, h, hr = refs[:m], refs[m : m + n], refs[m + n : m + 2 * n]
    outs = refs[-2:]
    for j, blocks in enumerate((h, hr)):
        total = refs[m + 2 * n + j][...] if has_acc else None
        b = 0
        for piece, cut in zip(pieces, cuts):
            for start in cut:
                part = jnp.dot(
                    blocks[b][...],
                    piece[start : start + PAIR],
                    preferred_element_type=jnp.float32,
                )
                total = part if total is None else total + part
                b += 1
        outs[j][...] = total


def values_part(pieces, acc):
    cuts = [[start for start, _, _ in parts] for _, parts in pieces]
    use = [(source, pair) for _, parts in pieces for _, source, pair in parts]
    t = use[0][0][0].shape[0]
    k = pieces[0][0].shape[1]
    acc = list(acc or ())
    whole = pl.BlockSpec((t, k), lambda i: (0, 0))
    columns = [pl.BlockSpec((t, PAIR), lambda i, p=p: (0, p)) for _, p in use]
    return pl.pallas_call(
        functools.partial(values_kernel, cuts, bool(acc)),
        grid=(1,),
        in_specs=[pl.BlockSpec(w.shape, lambda i: (0, 0)) for w, _ in pieces]
        + columns
        + columns
        + [whole] * len(acc),
        out_specs=[whole, whole],
        out_shape=[jax.ShapeDtypeStruct((t, k), jnp.float32)] * 2,
        compiler_params=params(),
        cost_estimate=FREE,
    )(
        *[w for w, _ in pieces],
        *[source[0] for source, _ in use],
        *[source[1] for source, _ in use],
        *acc,
    )


def encode_kernel(_, l_ref, g_ref, r_ref, keep, send):
    nudged = (g_ref[...] - l_ref[...]) + r_ref[...]
    top = jnp.max(jnp.abs(nudged), axis=1, keepdims=True) + 1e-06
    scale = top.astype(jnp.bfloat16).astype(jnp.float32)
    codes = (nudged / scale).astype(jnp.bfloat16).astype(jnp.float32)
    decoded = (codes * scale).astype(jnp.bfloat16)
    for half, out in enumerate((keep, send)):

        @pl.when(pl.program_id(0) // 2 == half)
        def _():
            out[...] = decoded


def encode(order, local_row, global_row, residual_row):
    n = local_row.shape[0] // RING
    part = pl.BlockSpec((n, BLOCK), lambda i, s: (s[i], 0))
    return pl.pallas_call(
        encode_kernel,
        grid_spec=pltpu.PrefetchScalarGridSpec(
            num_scalar_prefetch=1,
            grid=(RING,),
            in_specs=[part] * 3,
            out_specs=[
                pl.BlockSpec((n, BLOCK), lambda i, s: (jnp.minimum(i, 1), 0)),
                pl.BlockSpec((n, BLOCK), lambda i, s: (jnp.maximum(i - 2, 0), 0)),
            ],
        ),
        out_shape=[jax.ShapeDtypeStruct((2 * n, BLOCK), jnp.bfloat16)] * 2,
        compiler_params=params(),
        cost_estimate=FREE,
    )(order, local_row, global_row, residual_row)


def outer_kernel(replicas, _, l_ref, g_ref, m_ref, *refs):
    sums, (mixed_ref, momentum_ref) = refs[:-2], refs[-2:]
    for k, chunk in enumerate(sums):

        @pl.when(pl.program_id(0) == k)
        def _():
            average = chunk[...].astype(jnp.float32) / replicas
            new_momentum = outer_momentum * m_ref[...] + average
            new_global = g_ref[...] - outer_rate * (average + outer_momentum * new_momentum)
            mixed_ref[...] = mix_weight * l_ref[...] + (1.0 - mix_weight) * new_global
            momentum_ref[...] = new_momentum


def outer_step(order, replicas, local_row, global_row, momentum_row, sums):
    n = local_row.shape[0] // RING
    part = pl.BlockSpec((n, BLOCK), lambda i, s: (s[i], 0))
    first, second, pair = sums
    return pl.pallas_call(
        functools.partial(outer_kernel, replicas),
        grid_spec=pltpu.PrefetchScalarGridSpec(
            num_scalar_prefetch=1,
            grid=(RING,),
            in_specs=[part] * 3
            + [pl.BlockSpec((n, BLOCK), lambda i, s, b=b: (b, 0)) for b in (0, 0, 0, 1)],
            out_specs=[part, part],
        ),
        out_shape=[jax.ShapeDtypeStruct(local_row.shape, jnp.float32)] * 2,
        compiler_params=params(),
        cost_estimate=FREE,
    )(order, local_row, global_row, momentum_row, first, second, pair, pair)


def per_device(
    hidden_in, value_weight, grad_out, local_fragment, global_fragment, momentum, residual
):
    tokens = hidden_in[0]
    weight = value_weight[0]
    cot = grad_out[0]
    bf, f32 = jnp.bfloat16, jnp.float32
    x, y, zh, core = (lax.axis_index(a) for a in ("x", "y", "zh", "core"))

    def blocks(where):
        return [lax.rem(y + dy, RING) * RING + lax.rem(zh + dz, RING) for dy, dz in where]

    w_1, w_3 = shift(weight, "zh", -1), shift(weight, "zh", -3)

    mine, send = pick(tokens, core, blocks(FAR + NEXT + LAST), cot)
    local_row, global_row, momentum_row, residual_row = (
        v.reshape(-1, BLOCK) for v in (local_fragment, global_fragment, momentum, residual)
    )
    order = jnp.stack([x, x ^ 3, x ^ 1, x ^ 2])
    chunks = encode(order, local_row, global_row, residual_row)
    mine, send, w_1, w_3, *chunks = lax.optimization_barrier((mine, send, w_1, w_3, *chunks))
    theirs = shift(send, "core", 1)
    keep, to_pair = chunks
    from_pair = swap_x(to_pair, 1)

    w_2 = shift(after(weight, w_1), "zh", 2)
    w_01 = stack_rows(weight, w_1)
    prev_01, next_01 = shift(w_01, "y", 1), shift(w_01, "y", -1)

    def grads(first, dtypes, *others):
        return grad_rows_of(mine, after(theirs, *others), first, cot, theirs, dtypes)

    far_a, far_b = grads(0, [bf, bf], w_01)
    in_a, in_b = shift(far_a, "y", 1), shift(far_b, "y", -1)
    from_pair, prev_01, next_01 = after((from_pair, prev_01, next_01), far_a)
    dir_b, dir_a = grads(2, [bf, bf], from_pair, prev_01, next_01)
    keep, from_pair = after((keep, from_pair), dir_b)
    two = keep.astype(f32) + from_pair.astype(f32)
    n = two.shape[0] // 2
    from_other = swap_x(two[n:].astype(bf), 3)
    got_b, got_a = shift(dir_b, "y", 1), shift(dir_a, "y", -1)

    in_a, in_b, from_other = lax.optimization_barrier((in_a, in_b, from_other, dir_b))[:3]
    own_a, own_b, own_01, own_23 = grads(4, [f32] * 4, in_a, in_b, from_other)
    over_x = (two[:n] + after(from_other, own_a).astype(f32)).astype(bf)
    from_zl = shift(over_x, "zl", 1)
    prev_01, next_01 = after((prev_01, next_01), own_a)
    far_01 = shift(prev_01, "y", 1)
    in_a, in_b, got_a, got_b, w_2, from_zl = lax.optimization_barrier(
        (in_a, in_b, got_a, got_b, w_2, from_zl)
    )
    mer_a = (own_a + in_a.astype(f32)).astype(bf)
    mer_b = (own_b + in_b.astype(f32)).astype(bf)
    sum_a, sum_b = shift(mer_a, "y", 1), shift(mer_b, "y", -1)

    from_zl, over_x = after((from_zl, over_x), mer_a, mer_b)
    total = (over_x.astype(f32) + from_zl.astype(f32)).astype(bf)
    other_total = swap_x(total, 3)
    totals = total, other_total, swap_x(jnp.concatenate([total, other_total]), 1)
    replicas = lax.axis_size("x") * lax.axis_size("zl")
    mixed, new_momentum = outer_step(order, replicas, local_row, global_row, momentum_row, totals)

    w_23 = stack_rows(*after((w_2, w_3), mixed))
    far_01, *received = lax.optimization_barrier((far_01, got_a, sum_a, got_b, sum_b, w_23, mixed))[:5]
    up, down, own_up, own_down, own = sums_along_y(own_01, own_23, *received)
    from_below, from_above = shift(up, "zh", 1), shift(down, "zh", -1)
    w_23 = after(w_23, up)
    prev_23, next_23 = shift(w_23, "y", 1), shift(w_23, "y", -1)

    cols = (mine, theirs)
    acc = values_part(
        [
            (after(w_01, up), [(0, cols, 6)]),
            (w_23, [(0, cols, 7)]),
            (prev_01, [(0, cols, 3)]),
            (next_01, [(0, cols, 4)]),
            (far_01, [(0, cols, 0)]),
        ],
        None,
    )
    h = ROWS // 2
    mer_up = (own_up + from_below[:h].astype(f32)).astype(bf)
    mer_down = (own_down + from_above[:h].astype(f32)).astype(bf)
    top, bottom = shift(mer_up, "zh", 1), shift(mer_down, "zh", -1)
    prev_23, next_23 = after((prev_23, next_23), acc[0], mer_up, mer_down)
    far_23 = shift(next_23, "y", -1)
    acc = values_part([(prev_23, [(0, cols, 5)]), (next_23, [(0, cols, 2)])], acc)
    far_23, top, bottom = lax.optimization_barrier((far_23, top, bottom))
    ours, other = values_part([(far_23, [(0, cols, 1)])], acc)
    back = shift(other, "core", 1)
    direct = jnp.concatenate([from_above[h:], from_below[h:]]).astype(f32)
    grad_rows = own + direct + jnp.concatenate([top, bottom]).astype(f32)
    values = (ours + back).astype(bf)

    return (values[None], grad_rows[None], mixed.reshape(1, -1), new_momentum.reshape(-1))


def solution(mesh):
    whole = Mesh(mesh.devices.reshape(2, 4, 4, 4, 2), ("zl", "x", "y", "zh", "core"))
    replica, fsdp = ("zl", "x"), ("y", "zh", "core")
    return jax.shard_map(
        per_device,
        mesh=whole,
        in_specs=(
            P(replica, fsdp, None),
            P(replica, fsdp, None),
            P(replica, fsdp, None),
            P(replica, fsdp),
            P(fsdp),
            P(fsdp),
            P(replica, fsdp),
        ),
        out_specs=(
            P(replica, fsdp, None),
            P(replica, fsdp, None),
            P(replica, fsdp),
            P(fsdp),
        ),
        check_vma=False,
    )
```
